768 devices in a mesh: segment: 48 (over x, z), ctx: 8 (over y), head: 2 (over core).
Axes of the slice: x: 4, y: 8, z: 12, core: 2. Of those that a mesh axis runs over, the one named last changes fastest.
Arguments:
- inputs: bfloat16 [48, 1024, 5120], P('segment', 'ctx'), may hold values from -6 to 6
- query: bfloat16 [48, 1024, 20, 128], P('segment', 'ctx', 'head'), may hold values from -32 to 32
- grad_out: bfloat16 [48, 1024, 20, 128], P('segment', 'ctx', 'head'), may hold values from -6 to 6
- w_key: bfloat16 [48, 5120, 512], P('segment', None, 'head'), may hold values from -0.078125 to 0.078125
- w_value: bfloat16 [48, 5120, 512], P('segment', None, 'head'), may hold values from -0.078125 to 0.078125
- keep_mask: int32 [1024], replicated, may hold values from 0 to 1
Outputs:
- grad_input: float32 [48, 1024, 5120], P('segment', 'ctx', 'head')
The draws below stay inside these ranges and needn't reach their ends.
All inputs are finite; a program needn't handle non-finite values.
Results may differ from the reference program's by a relative error of at most 0.022.
The reference program's roundings to bfloat16 on the way (of `probs_b` and `dscore_b`) count: a program that leaves them out, or rounds other values in their place, can miss the bound.
Values may be sent and summed in bfloat16 or wider, within the bound.
A program may use at most 192 MiB of HBM per device.

```python
import math
import jax
import jax.numpy as jnp
from jax import lax

D = 5120
HEADS = 20
KV_HEADS = 4
HEAD_DIM = 128
SEQ = 1024
SEGMENTS = 48


def draw_query(key, part):
    first = jax.random.fold_in(key, 0)
    base = jax.random.normal(first, (SEGMENTS, SEQ, HEADS, HEAD_DIM), jnp.float32)
    return jnp.clip(base, -32.0, 32.0).astype(jnp.bfloat16)


def place_ends(result, rng, least, largest):
    longest = result.shape.index(max(result.shape))
    spots = []
    for shift in (0, 1):
        where = [jax.random.randint(jax.random.fold_in(rng, axis), (), 0, length) for axis, length in enumerate(result.shape)]
        where[longest] = (where[longest] + shift) % result.shape[longest]
        spots.append(tuple(where))
    return result.at[spots[0]].set(least).at[spots[1]].set(largest)


def level_of(stream_key, dims, pieces, low, top_value):
    level = 1.0
    for dim, blocks in pieces:
        steps = jax.random.uniform(jax.random.fold_in(jax.random.fold_in(stream_key, 6), dim), (blocks,), jnp.float32, low / len(pieces), top_value / len(pieces))
        level = level * jnp.repeat(jnp.exp(steps), dims[dim] // blocks).reshape((-1,) + (1,) * (len(dims) - 1 - dim))
    return level


def bell_draw(key, shape, deviation, bound, shards=(), kind=jnp.bfloat16):
    values = jax.random.normal(key, shape, jnp.float32) * deviation
    if len(shards) > 0:
        values = level_of(key, shape, shards, -0.22, 0.18) * values
    return jnp.clip(values, min=-bound, max=bound).astype(kind)


def setup_inputs(seed: int = 0) -> dict:
    splits = jax.random.split(jax.random.key(seed), 7)
    return {
        "inputs": bell_draw(splits[0], (SEGMENTS, SEQ, D), 1.0, 6.0, ((0, 48), (1, 8))),
        "query": draw_query(jax.random.fold_in(splits[6], 71), 0),
        "grad_out": bell_draw(splits[2], (SEGMENTS, SEQ, HEADS, HEAD_DIM), 1.0, 6.0, ((0, 48), (1, 8), (2, 2))),
        "w_key": bell_draw(splits[3], (SEGMENTS, D, KV_HEADS * HEAD_DIM), D ** -0.5, 0.078125, ((0, 48), (2, 2))),
        "w_value": bell_draw(splits[4], (SEGMENTS, D, KV_HEADS * HEAD_DIM), D ** -0.5, 0.078125, ((0, 48), (2, 2))),
        "keep_mask": place_ends(jax.random.randint(splits[5], (SEQ,), 0, 2), jax.random.fold_in(splits[5], 1), 0, 1).astype(jnp.int32),
    }


def one_section(xs, query_s, grad_s, wk, wv, keep_mask):
    seq_rows = xs.shape[0]
    group_size = HEADS // KV_HEADS
    scaling = 1.0 / math.sqrt(HEAD_DIM)
    key_rows = jnp.dot(xs, wk, preferred_element_type=jnp.float32).astype(jnp.bfloat16)
    value_rows = jnp.dot(xs, wv, preferred_element_type=jnp.float32).astype(jnp.bfloat16)
    key_heads = key_rows.reshape(seq_rows, KV_HEADS, HEAD_DIM).astype(jnp.float32)
    value_heads = value_rows.reshape(seq_rows, KV_HEADS, HEAD_DIM).astype(jnp.float32)
    query_heads = query_s.reshape(seq_rows, KV_HEADS, group_size, HEAD_DIM).astype(jnp.float32)
    grad_heads = grad_s.reshape(seq_rows, KV_HEADS, group_size, HEAD_DIM).astype(jnp.float32)
    scores = jnp.einsum('tkgd,skd->kgts', query_heads, key_heads) * scaling
    row_pos = jnp.arange(seq_rows, dtype=jnp.int32)[:, None]
    col_pos = jnp.arange(seq_rows, dtype=jnp.int32)[None, :]
    allowed = (col_pos <= row_pos) & ((keep_mask[None, :] == 1) | (col_pos == row_pos))
    masked = jnp.where(allowed, scores, -1e+30)
    top_score = lax.optimization_barrier(jnp.max(masked, axis=-1, keepdims=True))
    totals = lax.optimization_barrier(jnp.sum(jnp.where(allowed, jnp.exp(masked - top_score), 0.0), axis=-1, keepdims=True))
    log_total = top_score + jnp.log(totals)
    prob_full = jnp.where(allowed, jnp.exp(masked - log_total), 0.0)
    probs_b = lax.optimization_barrier(prob_full.astype(jnp.bfloat16)).astype(jnp.float32)
    attended = jnp.einsum('kgts,skd->tkgd', probs_b, value_heads)
    row_dots = lax.optimization_barrier(jnp.sum(grad_heads * attended, axis=-1))
    dprob = jnp.einsum('tkgd,skd->kgts', grad_heads, value_heads)
    dscore = prob_full * (dprob - jnp.transpose(row_dots, (1, 2, 0))[..., None])
    dscore_b = lax.optimization_barrier(dscore.astype(jnp.bfloat16)).astype(jnp.float32)
    grad_value = jnp.einsum('kgts,tkgd->skd', probs_b, grad_heads)
    grad_key = jnp.einsum('kgts,tkgd->skd', dscore_b, query_heads) * scaling
    grad_key = grad_key.reshape(seq_rows, KV_HEADS * HEAD_DIM).astype(jnp.bfloat16)
    grad_value = grad_value.reshape(seq_rows, KV_HEADS * HEAD_DIM).astype(jnp.bfloat16)
    contract = (((1,), (1,)), ((), ()))
    part_key = lax.dot_general(grad_key, wk, contract, preferred_element_type=jnp.float32)
    part_value = lax.dot_general(grad_value, wv, contract, preferred_element_type=jnp.float32)
    return part_key + part_value

def reference(inputs, query, grad_out, w_key, w_value, keep_mask):

    def section(packed):
        return one_section(packed[0], packed[1], packed[2], packed[3], packed[4], keep_mask)
    contribution = lax.map(section, (inputs, query, grad_out, w_key, w_value))
    return jnp.cumsum(contribution[::-1], axis=0)[::-1]
```

```python
import functools
import math

import jax
import jax.numpy as jnp
from jax import lax
from jax.experimental import pallas as pl
from jax.experimental.pallas import tpu as pltpu
from jax.sharding import PartitionSpec as P

MESH = pl.DeviceIdType.MESH
BF16 = jnp.bfloat16
F32 = jnp.float32
NX = 4
LAG = 5
ROW_ROW = (((1,), (1,)), ((), ()))


def fdot(a, b):
    return jnp.dot(a, b, preferred_element_type=F32)


def fdot_t(a, b):
    return lax.dot_general(a, b, ROW_ROW, preferred_element_type=F32)


def kernel_body(nz, nctx, x_ref, q_ref, g_ref, wk_ref, wv_ref, keep_ref, o_ref,
                kv, s_buf, dp_buf, rs_in, rs_out, grads, w_oth,
                d_buf, acc, u_in, r_in, l_in, u_out, r_out, l_out,
                ag_ss, ag_rs, rs_ss, rs_rs, w_ss, w_rs, h_ss, h_rs,
                u_ss, u_rs, r_ss, r_rs, l_ss, l_rs, o_sem):
    seg = lax.axis_index("segment")
    b = lax.axis_index("ctx")
    h = lax.axis_index("head")
    x = seg // nz
    z = seg - x * nz
    tok, width = x_ref.shape
    dim = kv.shape[3]
    rows = q_ref.shape[0] // 2
    heads = rows // tok
    half = w_oth.shape[1]
    scaling = 1.0 / math.sqrt(dim)
    xl = lax.rem(x + NX - 1, NX) * nz + z
    xr = lax.rem(x + 1, NX) * nz + z
    zl = x * nz + lax.rem(z + nz - 1, nz)
    zr = x * nz + lax.rem(z + 1, nz)
    yl = lax.rem(b + nctx - 1, nctx)
    yr = lax.rem(b + 1, nctx)

    barrier = pltpu.get_barrier_semaphore()
    for d in ({"segment": xl}, {"segment": xr}, {"segment": zl}, {"segment": zr},
              {"ctx": yl}, {"ctx": yr}, {"head": 1 - h}):
        pl.semaphore_signal(barrier, inc=1, device_id=d, device_id_type=MESH)
    pl.semaphore_wait(barrier, 7)

    def remote(src, dst, ss, rs, where):
        return pltpu.make_async_remote_copy(src, dst, ss, rs, device_id=where, device_id_type=MESH)

    theirs = pl.ds(pl.multiple_of((1 - h) * half, half), half)
    w_copies = [remote(w.at[theirs], w_oth.at[i], w_ss.at[i], w_rs.at[i], {"head": 1 - h})
                for i, w in enumerate((wk_ref, wv_ref))]
    for c in w_copies:
        c.start()

    step_k = 512

    def project(w_ref, i):
        at = pl.ds(pl.multiple_of(i * step_k, step_k), step_k)
        return fdot(x_ref[:, at], w_ref[at, :])

    def proj_step(i, carry):
        return carry[0] + project(wk_ref, i), carry[1] + project(wv_ref, i)
    zero = jnp.zeros((tok, 2 * dim), F32)
    key_rows, value_rows = lax.fori_loop(0, width // step_k, proj_step, (zero, zero))
    kv[b, 0] = key_rows[:, :dim].astype(BF16)
    kv[b, 1] = key_rows[:, dim:].astype(BF16)
    kv[b, 2] = value_rows[:, :dim].astype(BF16)
    kv[b, 3] = value_rows[:, dim:].astype(BF16)

    def up_copy(i, p):
        blk = lax.rem(b - i + nctx, nctx)
        return remote(kv.at[blk, p], kv.at[blk, p], ag_ss.at[i * 4 + p], ag_rs.at[i * 4 + p], {"ctx": yr})

    def up_got(i, p):
        blk = lax.rem(b - 1 - i + nctx, nctx)
        return remote(kv.at[blk, p], kv.at[blk, p], ag_ss.at[i * 4 + p], ag_rs.at[i * 4 + p], {"ctx": yr})

    def down_copy(i, p):
        blk = lax.rem(b + i, nctx)
        j = 16 + i * 4 + p
        return remote(kv.at[blk, p], kv.at[blk, p], ag_ss.at[j], ag_rs.at[j], {"ctx": yl})

    def down_got(i, p):
        blk = lax.rem(b + 1 + i, nctx)
        j = 16 + i * 4 + p
        return remote(kv.at[blk, p], kv.at[blk, p], ag_ss.at[j], ag_rs.at[j], {"ctx": yl})

    for p in range(4):
        up_copy(0, p).start()
        down_copy(0, p).start()

    def score_block(c, tops):
        key_pos = c * tok + lax.broadcasted_iota(jnp.int32, (tok, tok), 0)
        row_pos = b * tok + lax.broadcasted_iota(jnp.int32, (tok, tok), 1)
        at = pl.ds(pl.multiple_of(c * tok, tok), tok)
        kept = jnp.broadcast_to(keep_ref[at, :], (tok, tok))
        allowed = (key_pos <= row_pos) & ((kept == 1) | (key_pos == row_pos))
        limit = jnp.where(allowed, 3e38, -1e30)
        limit = jnp.concatenate([limit] * heads, axis=1)
        new = []
        for g in range(2):
            mine = pl.ds(g * rows, rows)
            s = fdot_t(kv[c, g], q_ref[mine, :]) * scaling
            s = jnp.minimum(s, limit)
            s_buf[g, at, :] = s
            dp_buf[g, at, :] = fdot_t(kv[c, 2 + g], g_ref[mine, :])
            new.append(jnp.maximum(tops[g], jnp.max(s, axis=0, keepdims=True)))
        return tuple(new)

    low = jnp.full((1, rows), -1e30, F32)
    tops = score_block(b, (low, low))

    def gather_step(i, tops):
        for p in range(4):
            up_got(i, p).wait_recv()

            @pl.when(i < 3)
            def _():
                up_copy(i + 1, p).start()

            @pl.when(i < 3)
            def _():
                down_got(i, p).wait_recv()

            @pl.when(i < 2)
            def _():
                down_copy(i + 1, p).start()
        tops = score_block(lax.rem(b - 1 - i + nctx, nctx), tops)
        return lax.cond(i < 3, lambda t: score_block(lax.rem(b + 1 + i, nctx), t), lambda t: t, tops)
    tops = lax.fori_loop(0, 4, gather_step, tops)

    def exp_step(c, sums):
        at = pl.ds(pl.multiple_of(c * tok, tok), tok)
        new = []
        for g in range(2):
            e = jnp.exp(s_buf[g, at, :] - tops[g])
            s_buf[g, at, :] = e
            new.append(sums[g] + jnp.sum(e, axis=0, keepdims=True))
        return tuple(new)
    none = jnp.zeros((1, rows), F32)
    sums = lax.fori_loop(0, nctx, exp_step, (none, none))
    inv = tuple(1.0 / s for s in sums)

    def dots_step(c, dots):
        at = pl.ds(pl.multiple_of(c * tok, tok), tok)
        new = []
        for g in range(2):
            prob = s_buf[g, at, :] * inv[g]
            s_buf[g, at, :] = prob
            low_prob = prob.astype(BF16).astype(F32)
            new.append(dots[g] + jnp.sum(low_prob * dp_buf[g, at, :], axis=0, keepdims=True))
        return tuple(new)
    dots = lax.fori_loop(0, nctx, dots_step, (none, none))

    def grad_block(c):
        at = pl.ds(pl.multiple_of(c * tok, tok), tok)
        out = [None] * 4
        for g in range(2):
            mine = pl.ds(g * rows, rows)
            prob = s_buf[g, at, :]
            ds = (prob * (dp_buf[g, at, :] - dots[g])).astype(BF16)
            out[g] = fdot(ds, q_ref[mine, :]) * scaling
            out[2 + g] = fdot(prob.astype(BF16), g_ref[mine, :])
        return out

    def rs_copy(j, p, where):
        k = j * 4 + p
        return remote(rs_out.at[k], rs_in.at[k], rs_ss.at[k], rs_rs.at[k], where)

    def rs_step(i, carry):
        part = grad_block(lax.rem(b + nctx - 4 + i, nctx))
        for p in range(4):
            k = i * 4 + p

            @pl.when(i > 0)
            def _():
                rs_copy(i - 1, p, {"ctx": yl}).wait_recv()
                rs_out[k] = (part[p] + rs_in[k - 4].astype(F32)).astype(BF16)

            @pl.when(i == 0)
            def _():
                rs_out[k] = part[p].astype(BF16)
            rs_copy(i, p, {"ctx": yl}).start()

        @pl.when(i < 3)
        def _():
            part = grad_block(lax.rem(b + 3 - i, nctx))
            for p in range(4):
                k = (4 + i) * 4 + p

                @pl.when(i > 0)
                def _():
                    rs_copy(3 + i, p, {"ctx": yr}).wait_recv()
                    rs_out[k] = (part[p] + rs_in[k - 4].astype(F32)).astype(BF16)

                @pl.when(i == 0)
                def _():
                    rs_out[k] = part[p].astype(BF16)
                rs_copy(4 + i, p, {"ctx": yr}).start()
        return carry
    lax.fori_loop(0, 4, rs_step, 0)
    part = grad_block(b)
    for p in range(4):
        rs_copy(6, p, {"ctx": yr}).wait_recv()
        rs_copy(3, p, {"ctx": yl}).wait_recv()
        total = part[p] + rs_in[24 + p].astype(F32) + rs_in[12 + p].astype(F32)
        grads[h, :, p * dim:(p + 1) * dim] = total.astype(BF16)
    h_copy = remote(grads.at[h], grads.at[h], h_ss, h_rs, {"head": 1 - h})
    h_copy.start()
    for c in w_copies:
        c.wait_recv()
    remote(grads.at[1 - h], grads.at[1 - h], h_ss, h_rs, {"head": 1 - h}).wait_recv()

    n, _, cols = d_buf.shape
    has_u = x < NX - 1
    off_r = (nz - 1 - z) * LAG
    off_l = z * LAG
    off_f = jnp.maximum(off_r, off_l)

    def u_copy(k):
        return remote(u_out.at[k], u_in.at[k], u_ss.at[k], u_rs.at[k], {"segment": xl})

    def r_copy(k):
        return remote(r_out.at[k], r_in.at[k], r_ss.at[k], r_rs.at[k], {"segment": zl})

    def l_copy(k):
        return remote(l_out.at[k], l_in.at[k], l_ss.at[k], l_rs.at[k], {"segment": zr})

    def o_copy(k):
        at = pl.ds(pl.multiple_of(k * cols, cols), cols)
        return pltpu.make_async_copy(acc.at[k], o_ref.at[:, at], o_sem.at[k])

    def contribution(k):
        own = pl.ds(pl.multiple_of(h * half + k * cols, cols), cols)
        oth = pl.ds(pl.multiple_of(k * cols, cols), cols)
        return (fdot_t(grads[h, :, :2 * dim], wk_ref[own, :]) + fdot_t(grads[h, :, 2 * dim:], wv_ref[own, :])
                + fdot_t(grads[1 - h, :, :2 * dim], w_oth[0, oth, :])
                + fdot_t(grads[1 - h, :, 2 * dim:], w_oth[1, oth, :]))

    def scan_step(t, carry):
        @pl.when(t < n)
        def _():
            k = t
            d_buf[k] = contribution(k)

            @pl.when(has_u)
            def _():
                u_copy(k).wait_recv()
                d_buf[k] = d_buf[k] + u_in[k].astype(F32)

            acc[k] = d_buf[k]

            @pl.when(x > 0)
            def _():
                u_out[k] = d_buf[k].astype(BF16)
                u_copy(k).start()

        k_r = t - off_r

        @pl.when((k_r >= 0) & (k_r < n))
        def _():
            k = k_r

            @pl.when(z < nz - 1)
            def _():
                r_copy(k).wait_recv()
                acc[k] = acc[k] + r_in[k].astype(F32)

            @pl.when((z > 0) & (z < nz - 1))
            def _():
                r_out[k] = (d_buf[k] + r_in[k].astype(F32)).astype(BF16)
                r_copy(k).start()

            @pl.when(z == nz - 1)
            def _():
                r_out[k] = d_buf[k].astype(BF16)
                r_copy(k).start()

        k_l = t - off_l

        @pl.when((k_l >= 0) & (k_l < n) & has_u)
        def _():
            k = k_l

            @pl.when(z > 0)
            def _():
                l_copy(k).wait_recv()
                acc[k] = acc[k] + l_in[k].astype(F32)

            @pl.when((z > 0) & (z < nz - 1))
            def _():
                l_out[k] = (u_in[k].astype(F32) + l_in[k].astype(F32)).astype(BF16)
                l_copy(k).start()

            @pl.when(z == 0)
            def _():
                l_out[k] = u_in[k]
                l_copy(k).start()

        k_f = t - off_f

        @pl.when((k_f >= 0) & (k_f < n))
        def _():
            o_copy(k_f).start()
        return carry
    lax.fori_loop(0, n + (nz - 1) * LAG, scan_step, 0)

    def drain(k, carry):
        o_copy(k).wait()

        @pl.when(x > 0)
        def _():
            u_copy(k).wait_send()

        @pl.when(z > 0)
        def _():
            r_copy(k).wait_send()

        @pl.when((z < nz - 1) & has_u)
        def _():
            l_copy(k).wait_send()
        return carry
    lax.fori_loop(0, n, drain, 0)
    for c in w_copies:
        c.wait_send()
    h_copy.wait_send()

    def drain_ctx(i, carry):
        for p in range(4):
            up_copy(i, p).wait_send()
            rs_copy(i, p, {"ctx": yl}).wait_send()

            @pl.when(i < 3)
            def _():
                down_copy(i, p).wait_send()
                rs_copy(4 + i, p, {"ctx": yr}).wait_send()
        return carry
    lax.fori_loop(0, 4, drain_ctx, 0)


def per_device(nz, nctx, inputs, query, grad_out, w_key, w_value, keep_mask):
    tok, width = inputs.shape[1:]
    heads, dim = query.shape[2:]
    half = width // 2
    cols = 128
    n = half // cols
    rows = heads * tok // 2
    seq = tok * nctx
    major = lambda a: jnp.moveaxis(a[0], 1, 0).reshape(heads * tok, dim)
    dma = pltpu.SemaphoreType.DMA
    out = pl.pallas_call(
        functools.partial(kernel_body, nz, nctx),
        out_shape=jax.ShapeDtypeStruct((tok, half), F32),
        in_specs=[pl.BlockSpec(memory_space=pltpu.VMEM)] * 6,
        out_specs=pl.BlockSpec(memory_space=pl.ANY),
        scratch_shapes=[
            pltpu.VMEM((nctx, 4, tok, dim), BF16),
            pltpu.VMEM((2, seq, rows), F32),
            pltpu.VMEM((2, seq, rows), F32),
            pltpu.VMEM((28, tok, dim), BF16),
            pltpu.VMEM((28, tok, dim), BF16),
            pltpu.VMEM((2, tok, 4 * dim), BF16),
            pltpu.VMEM((2, half, 2 * dim), BF16),
        ] + [pltpu.VMEM((n, tok, cols), F32)] * 2 + [pltpu.VMEM((n, tok, cols), BF16)] * 6
        + [dma((32,)), dma((32,)), dma((28,)), dma((28,)), dma((2,)), dma((2,)), dma, dma]
        + [dma((n,))] * 7,
        compiler_params=pltpu.CompilerParams(
            collective_id=0, has_side_effects=True, vmem_limit_bytes=56 * 2 ** 20),
        name="attention_backward_scan",
    )(inputs[0], major(query), major(grad_out), w_key[0], w_value[0], keep_mask.reshape(seq, 1))
    return out[None]


def solution(mesh):
    return jax.shard_map(
        functools.partial(per_device, mesh.shape["segment"] // NX, mesh.shape["ctx"]),
        mesh=mesh,
        in_specs=(
            P("segment", "ctx", None),
            P("segment", "ctx", "head", None),
            P("segment", "ctx", "head", None),
            P("segment", None, "head"),
            P("segment", None, "head"),
            P(),
        ),
        out_specs=P("segment", "ctx", "head"),
        check_vma=False,
    )
```

```python
import functools
import math

import jax
import jax.numpy as jnp
from jax import lax
from jax.experimental import pallas as pl
from jax.experimental.pallas import tpu as pltpu
from jax.sharding import PartitionSpec as P

MESH = pl.DeviceIdType.MESH
BF16 = jnp.bfloat16
F32 = jnp.float32
NX = 4
LAG = 5
LAGX = 5
PARTS = 2
COLS = 256
SUBS = 1
VMEM_MIB = 56
ROW_ROW = (((1,), (1,)), ((), ()))


def fdot(a, b):
    return jnp.dot(a, b, preferred_element_type=F32)


def fdot_t(a, b):
    return lax.dot_general(a, b, ROW_ROW, preferred_element_type=F32)


def kernel_body(nz, nctx, x_hbm, q_hbm, g_hbm, wk_hbm, wv_hbm, keep_ref, o_ref,
                q_ref, g_ref, x_ref, wk_ref, wv_ref, kv, e_buf, dp_buf, part, rs_in, rs_out, grads, w_oth,
                d_buf, u_buf, acc, a_in, b_in, r_in, l_in, a_out, b_out, r_out, l_out,
                in_sem, qg_sem, ag_ss, ag_rs, rs_ss, rs_rs, w_ss, w_rs, h_ss, h_rs,
                a_ss, a_rs, b_ss, b_rs, r_ss, r_rs, l_ss, l_rs, o_sem):
    seg = lax.axis_index("segment")
    b = lax.axis_index("ctx")
    h = lax.axis_index("head")
    x = seg // nz
    z = seg - x * nz
    tok, width = x_ref.shape
    dim = kv.shape[3]
    rows = q_ref.shape[0] // 2
    heads = rows // tok
    half = w_oth.shape[1]
    sub = tok // PARTS
    scaling = 1.0 / math.sqrt(dim)
    xl = lax.rem(x + NX - 1, NX) * nz + z
    xr = lax.rem(x + 1, NX) * nz + z
    zl = x * nz + lax.rem(z + nz - 1, nz)
    zr = x * nz + lax.rem(z + 1, nz)
    yl = lax.rem(b + nctx - 1, nctx)
    yr = lax.rem(b + 1, nctx)

    barrier = pltpu.get_barrier_semaphore()
    for d in ({"segment": xl}, {"segment": xr}, {"segment": zl}, {"segment": zr},
              {"ctx": yl}, {"ctx": yr}, {"head": 1 - h}):
        pl.semaphore_signal(barrier, inc=1, device_id=d, device_id_type=MESH)

    def remote(src, dst, ss, rs, where):
        return pltpu.make_async_remote_copy(src, dst, ss, rs, device_id=where, device_id_type=MESH)

    steps = in_sem.shape[0] // 3
    step_k = width // steps

    def loads(i):
        at = pl.ds(pl.multiple_of(i * step_k, step_k), step_k)
        return (pltpu.make_async_copy(x_hbm.at[:, at], x_ref.at[:, at], in_sem.at[3 * i]),
                pltpu.make_async_copy(wk_hbm.at[at], wk_ref.at[at], in_sem.at[3 * i + 1]),
                pltpu.make_async_copy(wv_hbm.at[at], wv_ref.at[at], in_sem.at[3 * i + 2]))
    for i in range(steps):
        for c in loads(i):
            c.start()
    qg_loads = [pltpu.make_async_copy(src, dst, qg_sem.at[i])
                for i, (src, dst) in enumerate(((q_hbm, q_ref), (g_hbm, g_ref)))]
    for c in qg_loads:
        c.start()

    def proj_step(i, carry):
        at = pl.ds(pl.multiple_of(i * step_k, step_k), step_k)
        for c in loads(i):
            c.wait()
        xs = x_ref[:, at]
        return carry[0] + fdot(xs, wk_ref[at, :]), carry[1] + fdot(xs, wv_ref[at, :])
    zero = jnp.zeros((tok, 2 * dim), F32)
    key_rows, value_rows = lax.fori_loop(0, steps, proj_step, (zero, zero))
    kv[b, 0] = key_rows[:, :dim].astype(BF16)
    kv[b, 1] = key_rows[:, dim:].astype(BF16)
    kv[b, 2] = value_rows[:, :dim].astype(BF16)
    kv[b, 3] = value_rows[:, dim:].astype(BF16)
    pl.semaphore_wait(barrier, 7)

    def up_copy(i, p):
        blk = lax.rem(b - i + nctx, nctx)
        return remote(kv.at[blk, p], kv.at[blk, p], ag_ss.at[i * 4 + p], ag_rs.at[i * 4 + p], {"ctx": yr})

    def up_got(i, p):
        blk = lax.rem(b - 1 - i + nctx, nctx)
        return remote(kv.at[blk, p], kv.at[blk, p], ag_ss.at[i * 4 + p], ag_rs.at[i * 4 + p], {"ctx": yr})

    def down_copy(i, p):
        blk = lax.rem(b + i, nctx)
        j = 16 + i * 4 + p
        return remote(kv.at[blk, p], kv.at[blk, p], ag_ss.at[j], ag_rs.at[j], {"ctx": yl})

    def down_got(i, p):
        blk = lax.rem(b + 1 + i, nctx)
        j = 16 + i * 4 + p
        return remote(kv.at[blk, p], kv.at[blk, p], ag_ss.at[j], ag_rs.at[j], {"ctx": yl})

    for p in range(4):
        up_copy(0, p).start()
        down_copy(0, p).start()

    theirs = pl.ds(pl.multiple_of((1 - h) * half, half), half)
    w_copies = [remote(w.at[theirs], w_oth.at[i], w_ss.at[i], w_rs.at[i], {"head": 1 - h})
                for i, w in enumerate((wk_ref, wv_ref))]
    for c in w_copies:
        c.start()

    def score_block(c, tops):
        key_pos = c * tok + lax.broadcasted_iota(jnp.int32, (tok, tok), 0)
        row_pos = b * tok + lax.broadcasted_iota(jnp.int32, (tok, tok), 1)
        this = lax.broadcasted_iota(jnp.int32, (nctx, tok), 0) == c
        kept = jnp.sum(jnp.where(this, keep_ref[...].astype(F32), 0.0), axis=0, keepdims=True)
        kept = jnp.broadcast_to(kept, (tok, tok)).T
        allowed = (key_pos <= row_pos) & ((kept == 1.0) | (key_pos == row_pos))
        limit = jnp.where(allowed, 3e38, -1e30)
        limit = jnp.concatenate([limit] * heads, axis=1)
        new = []
        for g in range(2):
            mine = pl.ds(g * rows, rows)
            s = fdot_t(kv[c, g], q_ref[mine, :]) * scaling
            s = jnp.minimum(s, limit)
            dp = fdot_t(kv[c, 2 + g], g_ref[mine, :])
            for p in range(PARTS):
                e_buf[g, p, c] = s[p * sub:(p + 1) * sub]
                dp_buf[g, p, c] = dp[p * sub:(p + 1) * sub]
            new.append(jnp.maximum(tops[g], jnp.max(s, axis=0, keepdims=True)))
        return tuple(new)

    for c in qg_loads:
        c.wait()
    low = jnp.full((1, rows), -1e30, F32)
    tops = score_block(b, (low, low))

    def gather_step(i, tops):
        for p in range(4):
            up_got(i, p).wait_recv()

            @pl.when(i < 3)
            def _():
                up_copy(i + 1, p).start()

            @pl.when(i < 3)
            def _():
                down_got(i, p).wait_recv()

            @pl.when(i < 2)
            def _():
                down_copy(i + 1, p).start()
        tops = score_block(lax.rem(b - 1 - i + nctx, nctx), tops)
        return lax.cond(i < 3, lambda t: score_block(lax.rem(b + 1 + i, nctx), t), lambda t: t, tops)
    tops = lax.fori_loop(0, 4, gather_step, tops)

    def exp_step(c, sums):
        new = []
        for g in range(2):
            total = sums[g]
            for p in range(PARTS):
                e = jnp.exp(e_buf[g, p, c] - tops[g])
                e_buf[g, p, c] = e
                total = total + jnp.sum(e, axis=0, keepdims=True)
            new.append(total)
        return tuple(new)
    none = jnp.zeros((1, rows), F32)
    sums = lax.fori_loop(0, nctx, exp_step, (none, none))
    inv = tuple(1.0 / s for s in sums)

    def dots_step(c, dots):
        new = []
        for g in range(2):
            total = dots[g]
            for p in range(PARTS):
                prob = e_buf[g, p, c] * inv[g]
                e_buf[g, p, c] = prob
                low_prob = prob.astype(BF16).astype(F32)
                total = total + jnp.sum(low_prob * dp_buf[g, p, c], axis=0, keepdims=True)
            new.append(total)
        return tuple(new)
    dots = lax.fori_loop(0, nctx, dots_step, (none, none))

    def make_part(p, q):
        for g in range(2):
            mine = pl.ds(g * rows, rows)
            prob = e_buf[g, p].reshape(nctx * sub, rows)
            if q == 0:
                out = fdot(prob.astype(BF16), g_ref[mine, :])
            else:
                dp = dp_buf[g, p].reshape(nctx * sub, rows)
                out = fdot((prob * (dp - dots[g])).astype(BF16), q_ref[mine, :]) * scaling
            part[p, q, :, :, g * dim:(g + 1) * dim] = out.reshape(nctx, sub, dim)

    def rs_copy(j, p, q):
        k = (j * PARTS + p) * 2 + q
        return remote(rs_out.at[k], rs_in.at[k], rs_ss.at[k], rs_rs.at[k], {"ctx": yl if j < 4 else yr})

    def rs_event(p, q, i):
        for j, blk in ((i, b + nctx - 4 + i), (4 + i, b + 3 - i)):
            if i == 3 and j == 7:
                continue
            k = (j * PARTS + p) * 2 + q
            val = part[p, q, lax.rem(blk, nctx)]
            if i > 0:
                rs_copy(j - 1, p, q).wait_recv()
                val = val + rs_in[k - 2 * PARTS].astype(F32)
            rs_out[k] = val.astype(BF16)
            rs_copy(j, p, q).start()

    def h_copy(p, who):
        at = pl.ds(p * sub, sub)
        return remote(grads.at[who, at], grads.at[who, at], h_ss.at[p], h_rs.at[p], {"head": 1 - h})

    def rs_final(p):
        for q in range(2):
            rs_copy(3, p, q).wait_recv()
            rs_copy(6, p, q).wait_recv()
            total = (part[p, q, b] + rs_in[(3 * PARTS + p) * 2 + q].astype(F32)
                     + rs_in[(6 * PARTS + p) * 2 + q].astype(F32))
            grads[h, p * sub:(p + 1) * sub, q * 2 * dim:(q + 1) * 2 * dim] = total.astype(BF16)
        h_copy(p, h).start()
        h_copy(p, 1 - h).wait_recv()

    for p in range(PARTS):
        for q in range(2):
            make_part(p, q)
            rs_event(p, q, 0)
    for i in range(1, 4):
        for p in range(PARTS):
            for q in range(2):
                rs_event(p, q, i)

    pieces, _, piece = d_buf.shape
    n = pieces // SUBS
    cols = piece * SUBS
    per = n // PARTS
    has_u = x < NX - 1
    off_u = jnp.where(x == NX - 1, 0, jnp.where(x == NX - 2, LAGX, 2 * LAGX))
    off_b = jnp.where(x == NX - 1, LAGX, off_u)
    off_r = off_u + (nz - 1 - z) * LAG
    off_l = off_u + z * LAG
    off_f = jnp.maximum(off_r, off_l)

    def a_copy(k):
        return remote(a_out.at[k], a_in.at[k], a_ss.at[k], a_rs.at[k], {"segment": xl})

    def b_copy(k):
        return remote(b_out.at[k], b_in.at[k], b_ss.at[k], b_rs.at[k], {"segment": xr})

    def r_copy(k):
        return remote(r_out.at[k], r_in.at[k], r_ss.at[k], r_rs.at[k], {"segment": zl})

    def l_copy(k):
        return remote(l_out.at[k], l_in.at[k], l_ss.at[k], l_rs.at[k], {"segment": zr})

    def o_copy(k):
        r = k // (per * SUBS)
        col = (k - r * per * SUBS) * piece
        return pltpu.make_async_copy(
            acc.at[k],
            o_ref.at[pl.ds(pl.multiple_of(r * sub, sub), sub), pl.ds(pl.multiple_of(col, piece), piece)],
            o_sem.at[k])

    def contribution(k):
        r = k // per
        col = (k - r * per) * cols
        own = pl.ds(pl.multiple_of(h * half + col, cols), cols)
        oth = pl.ds(pl.multiple_of(col, cols), cols)
        at = pl.ds(pl.multiple_of(r * sub, sub), sub)
        return (fdot_t(grads[h, at, :2 * dim], wv_ref[own, :]) + fdot_t(grads[h, at, 2 * dim:], wk_ref[own, :])
                + fdot_t(grads[1 - h, at, :2 * dim], w_oth[1, oth, :])
                + fdot_t(grads[1 - h, at, 2 * dim:], w_oth[0, oth, :]))

    def scan_step(t, carry):
        def turn(off, also=True):
            return (t >= off) & (t - off < n) & also

        def parts_of(off):
            return [(t - off) * SUBS + i for i in range(SUBS)]

        @pl.when(t < n)
        def _():
            c = contribution(t)
            for i, k in enumerate(parts_of(0)):
                d_buf[k] = c[:, i * piece:(i + 1) * piece]

            @pl.when((x == 3) | (x == 1))
            def _():
                for k in parts_of(0):
                    a_out[k] = d_buf[k].astype(BF16)
                    a_copy(k).start()

            @pl.when(x == 2)
            def _():
                for k in parts_of(0):
                    b_out[k] = d_buf[k].astype(BF16)
                    b_copy(k).start()

        @pl.when(turn(off_b, x == 3))
        def _():
            for k in parts_of(off_b):
                b_copy(k).wait_recv()
                b_out[k] = (d_buf[k] + b_in[k].astype(F32)).astype(BF16)
                b_copy(k).start()

        @pl.when(turn(off_u, x == 2))
        def _():
            for k in parts_of(off_u):
                a_copy(k).wait_recv()
                u_buf[k] = a_in[k].astype(F32)
                total = d_buf[k] + a_in[k].astype(F32)
                a_out[k] = total.astype(BF16)
                a_copy(k).start()
                d_buf[k] = total

        @pl.when(turn(off_u, x == 1))
        def _():
            for k in parts_of(off_u):
                a_copy(k).wait_recv()
                u_buf[k] = a_in[k].astype(F32)
                d_buf[k] = d_buf[k] + a_in[k].astype(F32)

        @pl.when(turn(off_u, x == 0))
        def _():
            for k in parts_of(off_u):
                a_copy(k).wait_recv()
                b_copy(k).wait_recv()
                u = a_in[k].astype(F32) + b_in[k].astype(F32)
                u_buf[k] = u
                d_buf[k] = d_buf[k] + u

        @pl.when(turn(off_r, z == nz - 1))
        def _():
            for k in parts_of(off_r):
                r_out[k] = d_buf[k].astype(BF16)
                r_copy(k).start()

        @pl.when(turn(off_r, (z > 0) & (z < nz - 1)))
        def _():
            for k in parts_of(off_r):
                r_copy(k).wait_recv()
                total = d_buf[k] + r_in[k].astype(F32)
                r_out[k] = total.astype(BF16)
                r_copy(k).start()

        @pl.when(turn(off_r, z == 0))
        def _():
            for k in parts_of(off_r):
                r_copy(k).wait_recv()

        @pl.when(turn(off_l, has_u & (z == 0)))
        def _():
            for k in parts_of(off_l):
                l_out[k] = u_buf[k].astype(BF16)
                l_copy(k).start()

        @pl.when(turn(off_l, has_u & (z > 0) & (z < nz - 1)))
        def _():
            for k in parts_of(off_l):
                l_copy(k).wait_recv()
                l_out[k] = (u_buf[k] + l_in[k].astype(F32)).astype(BF16)
                l_copy(k).start()

        @pl.when(turn(off_l, has_u & (z == nz - 1)))
        def _():
            for k in parts_of(off_l):
                l_copy(k).wait_recv()

        @pl.when(turn(off_f))
        def _():
            for k in parts_of(off_f):
                acc[k] = d_buf[k]

                @pl.when(z < nz - 1)
                def _():
                    acc[k] = acc[k] + r_in[k].astype(F32)

                @pl.when((z > 0) & has_u)
                def _():
                    acc[k] = acc[k] + l_in[k].astype(F32)
                o_copy(k).start()
        return carry

    rs_final(0)
    for c in w_copies:
        c.wait_recv()
    for p in range(PARTS - 1):
        lax.fori_loop(p * per, (p + 1) * per, scan_step, 0)
        rs_final(p + 1)
    lax.fori_loop((PARTS - 1) * per, n + 2 * LAGX + (nz - 1) * LAG, scan_step, 0)

    def drain(k, carry):
        o_copy(k).wait()

        @pl.when(x > 0)
        def _():
            a_copy(k).wait_send()

        @pl.when(x > 1)
        def _():
            b_copy(k).wait_send()

        @pl.when(z > 0)
        def _():
            r_copy(k).wait_send()

        @pl.when((z < nz - 1) & has_u)
        def _():
            l_copy(k).wait_send()
        return carry
    lax.fori_loop(0, pieces, drain, 0)
    for c in w_copies:
        c.wait_send()
    for p in range(PARTS):
        h_copy(p, h).wait_send()
        for q in range(2):
            for j in range(7):
                rs_copy(j, p, q).wait_send()

    def drain_ctx(i, carry):
        for p in range(4):
            up_copy(i, p).wait_send()

            @pl.when(i < 3)
            def _():
                down_copy(i, p).wait_send()
        return carry
    lax.fori_loop(0, 4, drain_ctx, 0)


def per_device(nz, nctx, inputs, query, grad_out, w_key, w_value, keep_mask):
    tok, width = inputs.shape[1:]
    heads, dim = query.shape[2:]
    half = width // 2
    cols = COLS
    n = half // cols * PARTS
    sub = tok // PARTS
    rows = heads * tok // 2
    kv_cols = w_key.shape[2]
    major = lambda a: jnp.moveaxis(a[0], 1, 0).reshape(heads * tok, dim)
    dma = pltpu.SemaphoreType.DMA
    vmem = pl.BlockSpec(memory_space=pltpu.VMEM)
    hbm = pl.BlockSpec(memory_space=pltpu.HBM)
    nrs = 7 * PARTS * 2
    out = pl.pallas_call(
        functools.partial(kernel_body, nz, nctx),
        out_shape=jax.ShapeDtypeStruct((tok, half), F32),
        in_specs=[hbm, hbm, hbm, hbm, hbm, vmem],
        out_specs=pl.BlockSpec(memory_space=pl.ANY),
        scratch_shapes=[
            pltpu.VMEM((heads * tok, dim), BF16),
            pltpu.VMEM((heads * tok, dim), BF16),
            pltpu.VMEM((tok, width), BF16),
            pltpu.VMEM((width, kv_cols), BF16),
            pltpu.VMEM((width, kv_cols), BF16),
            pltpu.VMEM((nctx, 4, tok, dim), BF16),
            pltpu.VMEM((2, PARTS, nctx, sub, rows), F32),
            pltpu.VMEM((2, PARTS, nctx, sub, rows), F32),
            pltpu.VMEM((PARTS, 2, nctx, sub, 2 * dim), F32),
            pltpu.VMEM((nrs, sub, 2 * dim), BF16),
            pltpu.VMEM((nrs, sub, 2 * dim), BF16),
            pltpu.VMEM((2, tok, 4 * dim), BF16),
            pltpu.VMEM((2, half, 2 * dim), BF16),
        ] + [pltpu.VMEM((n * SUBS, sub, cols // SUBS), F32)] * 3 + [pltpu.VMEM((n * SUBS, sub, cols // SUBS), BF16)] * 8
        + [dma((15,)), dma((2,)), dma((32,)), dma((32,)), dma((nrs,)), dma((nrs,)), dma((2,)), dma((2,)), dma((PARTS,)), dma((PARTS,))]
        + [dma((n * SUBS,))] * 9,
        compiler_params=pltpu.CompilerParams(
            collective_id=0, has_side_effects=True, vmem_limit_bytes=VMEM_MIB * 2 ** 20),
        name="attention_backward_scan",
    )(inputs[0], major(query), major(grad_out), w_key[0], w_value[0], keep_mask.reshape(nctx, tok))
    return out[None]


def solution(mesh):
    return jax.shard_map(
        functools.partial(per_device, mesh.shape["segment"] // NX, mesh.shape["ctx"]),
        mesh=mesh,
        in_specs=(
            P("segment", "ctx", None),
            P("segment", "ctx", "head", None),
            P("segment", "ctx", "head", None),
            P("segment", None, "head"),
            P("segment", None, "head"),
            P(),
        ),
        out_specs=P("segment", "ctx", "head"),
        check_vma=False,
    )
```

```python
import functools
import math

import jax
import jax.numpy as jnp
from jax import lax
from jax.experimental import pallas as pl
from jax.experimental.pallas import tpu as pltpu
from jax.sharding import PartitionSpec as P

MESH = pl.DeviceIdType.MESH
BF16 = jnp.bfloat16
F32 = jnp.float32
NX = 4
LAG = 5
LAGX = 5
PARTS = 2
COLS = 256
SUBS = 1
VMEM_MIB = 56
HELD = 3
PIECES = 4
ROW_ROW = (((1,), (1,)), ((), ()))


def fdot(a, b):
    return jnp.dot(a, b, preferred_element_type=F32)


def fdot_t(a, b):
    return lax.dot_general(a, b, ROW_ROW, preferred_element_type=F32)


def kernel_body(nz, nctx, x_hbm, q_hbm, g_hbm, wk_hbm, wv_hbm, keep_ref, o_ref,
                q_ref, g_ref, x_ref, wk_ref, wv_ref, kv, e_buf, dp_buf, part, rs_in, rs_out, grads, w_oth,
                d_buf, u_buf, acc, a_in, b_in, r_in, l_in, a_out, b_out, r_out, l_out,
                in_sem, qg_sem, ag_ss, ag_rs, rs_ss, rs_rs, w_ss, w_rs, h_ss, h_rs,
                a_ss, a_rs, b_ss, b_rs, r_ss, r_rs, l_ss, l_rs, o_sem):
    seg = lax.axis_index("segment")
    b = lax.axis_index("ctx")
    h = lax.axis_index("head")
    x = seg // nz
    z = seg - x * nz
    tok, width = x_ref.shape
    dim = kv.shape[3]
    rows = q_ref.shape[0] // 2
    heads = rows // tok
    half = w_oth.shape[1]
    sub = tok // PARTS
    scaling = 1.0 / math.sqrt(dim)
    xl = lax.rem(x + NX - 1, NX) * nz + z
    xr = lax.rem(x + 1, NX) * nz + z
    zl = x * nz + lax.rem(z + nz - 1, nz)
    zr = x * nz + lax.rem(z + 1, nz)
    yl = lax.rem(b + nctx - 1, nctx)
    yr = lax.rem(b + 1, nctx)

    barrier = pltpu.get_barrier_semaphore()
    for d in ({"segment": xl}, {"segment": xr}, {"segment": zl}, {"segment": zr},
              {"ctx": yl}, {"ctx": yr}, {"head": 1 - h}):
        pl.semaphore_signal(barrier, inc=1, device_id=d, device_id_type=MESH)

    def remote(src, dst, ss, rs, where):
        return pltpu.make_async_remote_copy(src, dst, ss, rs, device_id=where, device_id_type=MESH)

    steps = in_sem.shape[0] // 3
    step_k = width // steps

    def load(i, j):
        at = pl.ds(pl.multiple_of(i * step_k, step_k), step_k)
        src, dst = ((x_hbm.at[:, at], x_ref.at[:, at]), (wk_hbm.at[at], wk_ref.at[at]), (wv_hbm.at[at], wv_ref.at[at]))[j]
        return pltpu.make_async_copy(src, dst, in_sem.at[3 * i + j])
    for i in range(steps):
        load(i, 0).start()
        load(i, 1).start()
    for i in range(steps):
        load(i, 2).start()
    qg_loads = [pltpu.make_async_copy(src, dst, qg_sem.at[i])
                for i, (src, dst) in enumerate(((q_hbm, q_ref), (g_hbm, g_ref)))]
    for c in qg_loads:
        c.start()

    def project(w_ref, waits, at_kv):
        def proj_step(i, total):
            at = pl.ds(pl.multiple_of(i * step_k, step_k), step_k)
            for j in waits:
                load(i, j).wait()
            return total + fdot(x_ref[:, at], w_ref[at, :])
        out = lax.fori_loop(0, steps, proj_step, jnp.zeros((tok, 2 * dim), F32))
        kv[b, at_kv] = out[:, :dim].astype(BF16)
        kv[b, at_kv + 1] = out[:, dim:].astype(BF16)

    def ctx_copy(blk, p, j, where):
        at = pl.ds(p * (4 // PIECES), 4 // PIECES)
        return remote(kv.at[blk, at], kv.at[blk, at], ag_ss.at[j + p], ag_rs.at[j + p], where)

    def up_copy(i, p):
        return ctx_copy(lax.rem(b - i + nctx, nctx), p, i * PIECES, {"ctx": yr})

    def up_got(i, p):
        return ctx_copy(lax.rem(b - 1 - i + nctx, nctx), p, i * PIECES, {"ctx": yr})

    def down_copy(i, p):
        return ctx_copy(lax.rem(b + i, nctx), p, (4 + i) * PIECES, {"ctx": yl})

    def down_got(i, p):
        return ctx_copy(lax.rem(b + 1 + i, nctx), p, (4 + i) * PIECES, {"ctx": yl})

    project(wk_ref, (0, 1), 0)
    pl.semaphore_wait(barrier, 7)
    for p in range(PIECES // 2):
        up_copy(0, p).start()
        down_copy(0, p).start()
    project(wv_ref, (2,), 2)
    for p in range(PIECES // 2, PIECES):
        up_copy(0, p).start()
        down_copy(0, p).start()

    theirs = pl.ds(pl.multiple_of((1 - h) * half, half), half)
    w_copies = [remote(w.at[theirs], w_oth.at[i], w_ss.at[i], w_rs.at[i], {"head": 1 - h})
                for i, w in enumerate((wk_ref, wv_ref))]
    for c in w_copies:
        c.start()

    def score_block(c, tops):
        key_pos = c * tok + lax.broadcasted_iota(jnp.int32, (tok, tok), 0)
        row_pos = b * tok + lax.broadcasted_iota(jnp.int32, (tok, tok), 1)
        this = lax.broadcasted_iota(jnp.int32, (nctx, tok), 0) == c
        kept = jnp.sum(jnp.where(this, keep_ref[...].astype(F32), 0.0), axis=0, keepdims=True)
        kept = jnp.broadcast_to(kept, (tok, tok)).T
        allowed = (key_pos <= row_pos) & ((kept == 1.0) | (key_pos == row_pos))
        limit = jnp.where(allowed, 3e38, -1e30)
        limit = jnp.concatenate([limit] * heads, axis=1)
        new = []
        for g in range(2):
            mine = pl.ds(g * rows, rows)
            s = fdot_t(kv[c, g], q_ref[mine, :]) * scaling
            s = jnp.minimum(s, limit)
            dp = fdot_t(kv[c, 2 + g], g_ref[mine, :])
            for p in range(PARTS):
                e_buf[g, p, c] = s[p * sub:(p + 1) * sub]
                dp_buf[g, p, c] = dp[p * sub:(p + 1) * sub]
            new.append(jnp.maximum(tops[g], jnp.max(s, axis=0, keepdims=True)))
        return tuple(new)

    for c in qg_loads:
        c.wait()
    low = jnp.full((1, rows), -1e30, F32)
    tops = score_block(b, (low, low))

    def gather_step(i, tops):
        for p in range(PIECES):
            up_got(i, p).wait_recv()

            @pl.when(i < 3)
            def _():
                up_copy(i + 1, p).start()

            @pl.when(i < 3)
            def _():
                down_got(i, p).wait_recv()

            @pl.when(i < 2)
            def _():
                down_copy(i + 1, p).start()
        tops = score_block(lax.rem(b - 1 - i + nctx, nctx), tops)
        return lax.cond(i < 3, lambda t: score_block(lax.rem(b + 1 + i, nctx), t), lambda t: t, tops)
    tops = lax.fori_loop(0, 4, gather_step, tops)

    def exp_step(c, sums):
        new = []
        for g in range(2):
            total = sums[g]
            for p in range(PARTS):
                e = jnp.exp(e_buf[g, p, c] - tops[g])
                e_buf[g, p, c] = e
                total = total + jnp.sum(e, axis=0, keepdims=True)
            new.append(total)
        return tuple(new)
    none = jnp.zeros((1, rows), F32)
    sums = lax.fori_loop(0, nctx, exp_step, (none, none))
    inv = tuple(1.0 / s for s in sums)

    def dots_step(c, dots):
        new = []
        for g in range(2):
            total = dots[g]
            for p in range(PARTS):
                prob = e_buf[g, p, c] * inv[g]
                e_buf[g, p, c] = prob
                low_prob = prob.astype(BF16).astype(F32)
                total = total + jnp.sum(low_prob * dp_buf[g, p, c], axis=0, keepdims=True)
            new.append(total)
        return tuple(new)
    dots = lax.fori_loop(0, nctx, dots_step, (none, none))

    def make_part(p, q):
        for g in range(2):
            mine = pl.ds(g * rows, rows)
            prob = e_buf[g, p].reshape(nctx * sub, rows)
            if q == 0:
                out = fdot(prob.astype(BF16), g_ref[mine, :])
            else:
                dp = dp_buf[g, p].reshape(nctx * sub, rows)
                out = fdot((prob * (dp - dots[g])).astype(BF16), q_ref[mine, :]) * scaling
            part[p, q, :, :, g * dim:(g + 1) * dim] = out.reshape(nctx, sub, dim)

    def rs_copy(j, p, q):
        k = (j * PARTS + p) * 2 + q
        return remote(rs_out.at[k], rs_in.at[k], rs_ss.at[k], rs_rs.at[k], {"ctx": yl if j < 4 else yr})

    def rs_event(p, q, i):
        for j, blk in ((i, b + nctx - 4 + i), (4 + i, b + 3 - i)):
            if i == 3 and j == 7:
                continue
            k = (j * PARTS + p) * 2 + q
            val = part[p, q, lax.rem(blk, nctx)]
            if i > 0:
                rs_copy(j - 1, p, q).wait_recv()
                val = val + rs_in[k - 2 * PARTS].astype(F32)
            rs_out[k] = val.astype(BF16)
            rs_copy(j, p, q).start()

    def h_copy(p, who):
        at = pl.ds(p * sub, sub)
        return remote(grads.at[who, at], grads.at[who, at], h_ss.at[p], h_rs.at[p], {"head": 1 - h})

    def rs_final(p):
        for q in range(2):
            rs_copy(3, p, q).wait_recv()
            rs_copy(6, p, q).wait_recv()
            total = (part[p, q, b] + rs_in[(3 * PARTS + p) * 2 + q].astype(F32)
                     + rs_in[(6 * PARTS + p) * 2 + q].astype(F32))
            grads[h, p * sub:(p + 1) * sub, q * 2 * dim:(q + 1) * 2 * dim] = total.astype(BF16)
        h_copy(p, h).start()
        h_copy(p, 1 - h).wait_recv()

    for p in range(PARTS):
        for q in range(2):
            make_part(p, q)
            rs_event(p, q, 0)
    for i in range(1, 4):
        for p in range(PARTS):
            for q in range(2):
                rs_event(p, q, i)

    pieces, _, piece = d_buf.shape
    n = pieces // SUBS
    cols = piece * SUBS
    per = n // PARTS
    has_u = x < NX - 1
    off_u = jnp.where(x == NX - 1, 0, jnp.where(x == NX - 2, LAGX, 2 * LAGX))
    off_b = jnp.where(x == NX - 1, LAGX, off_u)
    off_r = off_u + (nz - 1 - z) * LAG
    off_l = off_u + z * LAG
    off_f = jnp.maximum(off_r, off_l)

    def a_copy(k):
        return remote(a_out.at[k], a_in.at[k], a_ss.at[k], a_rs.at[k], {"segment": xl})

    def b_copy(k):
        return remote(b_out.at[k], b_in.at[k], b_ss.at[k], b_rs.at[k], {"segment": xr})

    def r_copy(k):
        return remote(r_out.at[k], r_in.at[k], r_ss.at[k], r_rs.at[k], {"segment": zl})

    def l_copy(k):
        return remote(l_out.at[k], l_in.at[k], l_ss.at[k], l_rs.at[k], {"segment": zr})

    def o_copy(k):
        r = k // (per * SUBS)
        col = (k - r * per * SUBS) * piece
        return pltpu.make_async_copy(
            acc.at[k],
            o_ref.at[pl.ds(pl.multiple_of(r * sub, sub), sub), pl.ds(pl.multiple_of(col, piece), piece)],
            o_sem.at[k])

    def contribution(k):
        r = k // per
        col = (k - r * per) * cols
        own = pl.ds(pl.multiple_of(h * half + col, cols), cols)
        oth = pl.ds(pl.multiple_of(col, cols), cols)
        at = pl.ds(pl.multiple_of(r * sub, sub), sub)
        return (fdot_t(grads[h, at, :2 * dim], wv_ref[own, :]) + fdot_t(grads[h, at, 2 * dim:], wk_ref[own, :])
                + fdot_t(grads[1 - h, at, :2 * dim], w_oth[1, oth, :])
                + fdot_t(grads[1 - h, at, 2 * dim:], w_oth[0, oth, :]))

    ends = (z == 0) | (z == nz - 1)

    def drain_sends():
        def drain(k, carry):
            @pl.when(x > 0)
            def _():
                a_copy(k).wait_send()

            @pl.when(x > 1)
            def _():
                b_copy(k).wait_send()

            @pl.when(z > 0)
            def _():
                r_copy(k).wait_send()

            @pl.when((z < nz - 1) & has_u)
            def _():
                l_copy(k).wait_send()
            return carry
        lax.fori_loop(0, pieces, drain, 0)
        for c in w_copies:
            c.wait_send()
        for p in range(PARTS):
            h_copy(p, h).wait_send()
            for q in range(2):
                for j in range(7):
                    rs_copy(j, p, q).wait_send()

        def drain_ctx(i, carry):
            for p in range(PIECES):
                up_copy(i, p).wait_send()

                @pl.when(i < 3)
                def _():
                    down_copy(i, p).wait_send()
            return carry
        lax.fori_loop(0, 4, drain_ctx, 0)

    def scan_step(t, carry):
        @pl.when(ends & (t == off_f - 2))
        def _():
            drain_sends()

        def turn(off, also=True):
            return (t >= off) & (t - off < n) & also

        def parts_of(off):
            return [(t - off) * SUBS + i for i in range(SUBS)]

        @pl.when(t < n)
        def _():
            c = contribution(t)
            for i, k in enumerate(parts_of(0)):
                d_buf[k] = c[:, i * piece:(i + 1) * piece]

            @pl.when((x == 3) | (x == 1))
            def _():
                for k in parts_of(0):
                    a_out[k] = d_buf[k].astype(BF16)
                    a_copy(k).start()

            @pl.when(x == 2)
            def _():
                for k in parts_of(0):
                    b_out[k] = d_buf[k].astype(BF16)
                    b_copy(k).start()

        @pl.when(turn(off_b, x == 3))
        def _():
            for k in parts_of(off_b):
                b_copy(k).wait_recv()
                b_out[k] = (d_buf[k] + b_in[k].astype(F32)).astype(BF16)
                b_copy(k).start()

        @pl.when(turn(off_u, x == 2))
        def _():
            for k in parts_of(off_u):
                a_copy(k).wait_recv()
                u_buf[k] = a_in[k].astype(F32)
                total = d_buf[k] + a_in[k].astype(F32)
                a_out[k] = total.astype(BF16)
                a_copy(k).start()
                d_buf[k] = total

        @pl.when(turn(off_u, x == 1))
        def _():
            for k in parts_of(off_u):
                a_copy(k).wait_recv()
                u_buf[k] = a_in[k].astype(F32)
                d_buf[k] = d_buf[k] + a_in[k].astype(F32)

        @pl.when(turn(off_u, x == 0))
        def _():
            for k in parts_of(off_u):
                a_copy(k).wait_recv()
                b_copy(k).wait_recv()
                u = a_in[k].astype(F32) + b_in[k].astype(F32)
                u_buf[k] = u
                d_buf[k] = d_buf[k] + u

        @pl.when(turn(off_r, z == nz - 1))
        def _():
            for k in parts_of(off_r):
                r_out[k] = d_buf[k].astype(BF16)
                r_copy(k).start()

        @pl.when(turn(off_r, (z > 0) & (z < nz - 1)))
        def _():
            for k in parts_of(off_r):
                r_copy(k).wait_recv()
                total = d_buf[k] + r_in[k].astype(F32)
                r_out[k] = total.astype(BF16)
                r_copy(k).start()

        @pl.when(turn(off_r, z == 0))
        def _():
            for k in parts_of(off_r):
                r_copy(k).wait_recv()

        @pl.when(turn(off_l, has_u & (z == 0)))
        def _():
            for k in parts_of(off_l):
                l_out[k] = u_buf[k].astype(BF16)
                l_copy(k).start()

        @pl.when(turn(off_l, has_u & (z > 0) & (z < nz - 1)))
        def _():
            for k in parts_of(off_l):
                l_copy(k).wait_recv()
                l_out[k] = (u_buf[k] + l_in[k].astype(F32)).astype(BF16)
                l_copy(k).start()

        @pl.when(turn(off_l, has_u & (z == nz - 1)))
        def _():
            for k in parts_of(off_l):
                l_copy(k).wait_recv()

        @pl.when(turn(off_f))
        def _():
            for k in parts_of(off_f):
                acc[k] = d_buf[k]

                @pl.when(z < nz - 1)
                def _():
                    acc[k] = acc[k] + r_in[k].astype(F32)

                @pl.when((z > 0) & has_u)
                def _():
                    acc[k] = acc[k] + l_in[k].astype(F32)
                o_copy(k).start()

                @pl.when(k >= HELD)
                def _():
                    o_copy(k - HELD).wait()
        return carry

    rs_final(0)
    for c in w_copies:
        c.wait_recv()
    for p in range(PARTS - 1):
        lax.fori_loop(p * per, (p + 1) * per, scan_step, 0)
        rs_final(p + 1)
    lax.fori_loop((PARTS - 1) * per, n + 2 * LAGX + (nz - 1) * LAG, scan_step, 0)

    @pl.when(jnp.logical_not(ends))
    def _():
        drain_sends()

    def drain_out(k, carry):
        o_copy(k).wait()
        return carry
    lax.fori_loop(pieces - HELD, pieces, drain_out, 0)


def per_device(nz, nctx, inputs, query, grad_out, w_key, w_value, keep_mask):
    tok, width = inputs.shape[1:]
    heads, dim = query.shape[2:]
    half = width // 2
    cols = COLS
    n = half // cols * PARTS
    sub = tok // PARTS
    rows = heads * tok // 2
    kv_cols = w_key.shape[2]
    major = lambda a: jnp.moveaxis(a[0], 1, 0).reshape(heads * tok, dim)
    dma = pltpu.SemaphoreType.DMA
    vmem = pl.BlockSpec(memory_space=pltpu.VMEM)
    hbm = pl.BlockSpec(memory_space=pltpu.HBM)
    nrs = 7 * PARTS * 2
    out = pl.pallas_call(
        functools.partial(kernel_body, nz, nctx),
        out_shape=jax.ShapeDtypeStruct((tok, half), F32),
        in_specs=[hbm, hbm, hbm, hbm, hbm, vmem],
        out_specs=pl.BlockSpec(memory_space=pl.ANY),
        scratch_shapes=[
            pltpu.VMEM((heads * tok, dim), BF16),
            pltpu.VMEM((heads * tok, dim), BF16),
            pltpu.VMEM((tok, width), BF16),
            pltpu.VMEM((width, kv_cols), BF16),
            pltpu.VMEM((width, kv_cols), BF16),
            pltpu.VMEM((nctx, 4, tok, dim), BF16),
            pltpu.VMEM((2, PARTS, nctx, sub, rows), F32),
            pltpu.VMEM((2, PARTS, nctx, sub, rows), F32),
            pltpu.VMEM((PARTS, 2, nctx, sub, 2 * dim), F32),
            pltpu.VMEM((nrs, sub, 2 * dim), BF16),
            pltpu.VMEM((nrs, sub, 2 * dim), BF16),
            pltpu.VMEM((2, tok, 4 * dim), BF16),
            pltpu.VMEM((2, half, 2 * dim), BF16),
        ] + [pltpu.VMEM((n * SUBS, sub, cols // SUBS), F32)] * 3 + [pltpu.VMEM((n * SUBS, sub, cols // SUBS), BF16)] * 8
        + [dma((15,)), dma((2,)), dma((8 * PIECES,)), dma((8 * PIECES,)), dma((nrs,)), dma((nrs,)), dma((2,)), dma((2,)), dma((PARTS,)), dma((PARTS,))]
        + [dma((n * SUBS,))] * 9,
        compiler_params=pltpu.CompilerParams(
            collective_id=0, has_side_effects=True, vmem_limit_bytes=VMEM_MIB * 2 ** 20),
        name="attention_backward_scan",
    )(inputs[0], major(query), major(grad_out), w_key[0], w_value[0], keep_mask.reshape(nctx, tok))
    return out[None]


def solution(mesh):
    return jax.shard_map(
        functools.partial(per_device, mesh.shape["segment"] // NX, mesh.shape["ctx"]),
        mesh=mesh,
        in_specs=(
            P("segment", "ctx", None),
            P("segment", "ctx", "head", None),
            P("segment", "ctx", "head", None),
            P("segment", None, "head"),
            P("segment", None, "head"),
            P(),
        ),
        out_specs=P("segment", "ctx", "head"),
        check_vma=False,
    )
```

```python
import functools
import math

import jax
import jax.numpy as jnp
from jax import lax
from jax.experimental import pallas as pl
from jax.experimental.pallas import tpu as pltpu
from jax.sharding import PartitionSpec as P

MESH = pl.DeviceIdType.MESH
BF16 = jnp.bfloat16
F32 = jnp.float32
NX = 4
LAG = 5
LAGX = 5
PARTS = 2
COLS = 256
SUBS = 1
VMEM_MIB = 56
HELD = 3
PIECES = 4
ROW_ROW = (((1,), (1,)), ((), ()))


def fdot(a, b):
    return jnp.dot(a, b, preferred_element_type=F32)


def fdot_t(a, b):
    return lax.dot_general(a, b, ROW_ROW, preferred_element_type=F32)


def kernel_body(nz, nctx, x_hbm, q_hbm, g_hbm, wk_hbm, wv_hbm, keep_ref, o_ref,
                q_ref, g_ref, x_ref, wk_ref, wv_ref, kv, e_buf, dp_buf, top_buf, sum_buf, part, rs_in, rs_out, grads, w_oth,
                d_buf, u_buf, acc, a_in, b_in, r_in, l_in, a_out, b_out, r_out, l_out,
                in_sem, qg_sem, ag_ss, ag_rs, rs_ss, rs_rs, w_ss, w_rs, h_ss, h_rs,
                a_ss, a_rs, b_ss, b_rs, r_ss, r_rs, l_ss, l_rs, o_sem):
    seg = lax.axis_index("segment")
    b = lax.axis_index("ctx")
    h = lax.axis_index("head")
    x = seg // nz
    z = seg - x * nz
    tok, width = x_ref.shape
    dim = kv.shape[3]
    rows = q_ref.shape[0] // 2
    heads = rows // tok
    half = w_oth.shape[1]
    sub = tok // PARTS
    scaling = 1.0 / math.sqrt(dim)
    xl = lax.rem(x + NX - 1, NX) * nz + z
    xr = lax.rem(x + 1, NX) * nz + z
    zl = x * nz + lax.rem(z + nz - 1, nz)
    zr = x * nz + lax.rem(z + 1, nz)
    yl = lax.rem(b + nctx - 1, nctx)
    yr = lax.rem(b + 1, nctx)

    barrier = pltpu.get_barrier_semaphore()
    for d in ({"segment": xl}, {"segment": xr}, {"segment": zl}, {"segment": zr},
              {"ctx": yl}, {"ctx": yr}, {"head": 1 - h}):
        pl.semaphore_signal(barrier, inc=1, device_id=d, device_id_type=MESH)

    def remote(src, dst, ss, rs, where):
        return pltpu.make_async_remote_copy(src, dst, ss, rs, device_id=where, device_id_type=MESH)

    steps = in_sem.shape[0] // 3
    step_k = width // steps

    def load(i, j):
        at = pl.ds(pl.multiple_of(i * step_k, step_k), step_k)
        src, dst = ((x_hbm.at[:, at], x_ref.at[:, at]), (wk_hbm.at[at], wk_ref.at[at]), (wv_hbm.at[at], wv_ref.at[at]))[j]
        return pltpu.make_async_copy(src, dst, in_sem.at[3 * i + j])
    for i in range(steps):
        load(i, 0).start()
        load(i, 1).start()
    for i in range(steps):
        load(i, 2).start()
    qg_loads = [pltpu.make_async_copy(src, dst, qg_sem.at[i])
                for i, (src, dst) in enumerate(((q_hbm, q_ref), (g_hbm, g_ref)))]
    for c in qg_loads:
        c.start()

    def project(w_ref, waits, at_kv):
        def proj_step(i, total):
            at = pl.ds(pl.multiple_of(i * step_k, step_k), step_k)
            for j in waits:
                load(i, j).wait()
            return total + fdot(x_ref[:, at], w_ref[at, :])
        out = lax.fori_loop(0, steps, proj_step, jnp.zeros((tok, 2 * dim), F32))
        kv[b, at_kv] = out[:, :dim].astype(BF16)
        kv[b, at_kv + 1] = out[:, dim:].astype(BF16)

    def ctx_copy(blk, p, j, where):
        at = pl.ds(p * (4 // PIECES), 4 // PIECES)
        return remote(kv.at[blk, at], kv.at[blk, at], ag_ss.at[j + p], ag_rs.at[j + p], where)

    def up_copy(i, p):
        return ctx_copy(lax.rem(b - i + nctx, nctx), p, i * PIECES, {"ctx": yr})

    def up_got(i, p):
        return ctx_copy(lax.rem(b - 1 - i + nctx, nctx), p, i * PIECES, {"ctx": yr})

    def down_copy(i, p):
        return ctx_copy(lax.rem(b + i, nctx), p, (4 + i) * PIECES, {"ctx": yl})

    def down_got(i, p):
        return ctx_copy(lax.rem(b + 1 + i, nctx), p, (4 + i) * PIECES, {"ctx": yl})

    project(wk_ref, (0, 1), 0)
    pl.semaphore_wait(barrier, 7)
    for p in range(PIECES // 2):
        up_copy(0, p).start()
        down_copy(0, p).start()
    project(wv_ref, (2,), 2)
    for p in range(PIECES // 2, PIECES):
        up_copy(0, p).start()
        down_copy(0, p).start()

    theirs = pl.ds(pl.multiple_of((1 - h) * half, half), half)
    w_copies = [remote(w.at[theirs], w_oth.at[i], w_ss.at[i], w_rs.at[i], {"head": 1 - h})
                for i, w in enumerate((wk_ref, wv_ref))]
    for c in w_copies:
        c.start()

    def score_block(c, tops):
        key_pos = c * tok + lax.broadcasted_iota(jnp.int32, (tok, tok), 0)
        row_pos = b * tok + lax.broadcasted_iota(jnp.int32, (tok, tok), 1)
        this = lax.broadcasted_iota(jnp.int32, (nctx, tok), 0) == c
        kept = jnp.sum(jnp.where(this, keep_ref[...].astype(F32), 0.0), axis=0, keepdims=True)
        kept = jnp.broadcast_to(kept, (tok, tok)).T
        allowed = (key_pos <= row_pos) & ((kept == 1.0) | (key_pos == row_pos))
        limit = jnp.where(allowed, 3e38, -1e30)
        limit = jnp.concatenate([limit] * heads, axis=1)
        new = []
        for g in range(2):
            mine = pl.ds(g * rows, rows)
            s = fdot_t(kv[c, g], q_ref[mine, :]) * scaling
            s = jnp.minimum(s, limit)
            dp = fdot_t(kv[c, 2 + g], g_ref[mine, :])
            top = jnp.max(s, axis=0, keepdims=True)
            e = jnp.exp(s - top)
            for p in range(PARTS):
                e_buf[g, p, c] = e[p * sub:(p + 1) * sub]
                dp_buf[g, p, c] = dp[p * sub:(p + 1) * sub]
            top_buf[c, g] = top
            sum_buf[c, g] = jnp.sum(e, axis=0, keepdims=True)
            new.append(jnp.maximum(tops[g], top))
        return tuple(new)

    for c in qg_loads:
        c.wait()
    low = jnp.full((1, rows), -1e30, F32)
    tops = score_block(b, (low, low))

    def gather_step(i, tops):
        for p in range(PIECES):
            up_got(i, p).wait_recv()

            @pl.when(i < 3)
            def _():
                up_copy(i + 1, p).start()

            @pl.when(i < 3)
            def _():
                down_got(i, p).wait_recv()

            @pl.when(i < 2)
            def _():
                down_copy(i + 1, p).start()
        tops = score_block(lax.rem(b - 1 - i + nctx, nctx), tops)
        return lax.cond(i < 3, lambda t: score_block(lax.rem(b + 1 + i, nctx), t), lambda t: t, tops)
    tops = lax.fori_loop(0, 4, gather_step, tops)

    def weigh_step(c, sums):
        new = []
        for g in range(2):
            weight = jnp.exp(top_buf[c, g] - tops[g])
            top_buf[c, g] = weight
            new.append(sums[g] + weight * sum_buf[c, g])
        return tuple(new)
    none = jnp.zeros((1, rows), F32)
    sums = lax.fori_loop(0, nctx, weigh_step, (none, none))
    inv = tuple(1.0 / s for s in sums)

    def dots_step(c, dots):
        new = []
        for g in range(2):
            total = dots[g]
            for p in range(PARTS):
                prob = e_buf[g, p, c] * (top_buf[c, g] * inv[g])
                e_buf[g, p, c] = prob
                low_prob = prob.astype(BF16).astype(F32)
                total = total + jnp.sum(low_prob * dp_buf[g, p, c], axis=0, keepdims=True)
            new.append(total)
        return tuple(new)
    dots = lax.fori_loop(0, nctx, dots_step, (none, none))

    def make_part(p, q):
        for g in range(2):
            mine = pl.ds(g * rows, rows)
            prob = e_buf[g, p].reshape(nctx * sub, rows)
            if q == 0:
                out = fdot(prob.astype(BF16), g_ref[mine, :])
            else:
                dp = dp_buf[g, p].reshape(nctx * sub, rows)
                out = fdot((prob * (dp - dots[g])).astype(BF16), q_ref[mine, :]) * scaling
            part[p, q, :, :, g * dim:(g + 1) * dim] = out.reshape(nctx, sub, dim)

    def rs_copy(j, p, q):
        k = (j * PARTS + p) * 2 + q
        return remote(rs_out.at[k], rs_in.at[k], rs_ss.at[k], rs_rs.at[k], {"ctx": yl if j < 4 else yr})

    def rs_event(p, q, i):
        for j, blk in ((i, b + nctx - 4 + i), (4 + i, b + 3 - i)):
            if i == 3 and j == 7:
                continue
            k = (j * PARTS + p) * 2 + q
            val = part[p, q, lax.rem(blk, nctx)]
            if i > 0:
                rs_copy(j - 1, p, q).wait_recv()
                val = val + rs_in[k - 2 * PARTS].astype(F32)
            rs_out[k] = val.astype(BF16)
            rs_copy(j, p, q).start()

    def h_copy(p, who):
        at = pl.ds(p * sub, sub)
        return remote(grads.at[who, at], grads.at[who, at], h_ss.at[p], h_rs.at[p], {"head": 1 - h})

    def rs_final(p):
        for q in range(2):
            rs_copy(3, p, q).wait_recv()
            rs_copy(6, p, q).wait_recv()
            total = (part[p, q, b] + rs_in[(3 * PARTS + p) * 2 + q].astype(F32)
                     + rs_in[(6 * PARTS + p) * 2 + q].astype(F32))
            grads[h, p * sub:(p + 1) * sub, q * 2 * dim:(q + 1) * 2 * dim] = total.astype(BF16)
        h_copy(p, h).start()
        h_copy(p, 1 - h).wait_recv()

    for p in range(PARTS):
        for q in range(2):
            make_part(p, q)
            rs_event(p, q, 0)
    for i in range(1, 4):
        for p in range(PARTS):
            for q in range(2):
                rs_event(p, q, i)

    pieces, _, piece = d_buf.shape
    n = pieces // SUBS
    cols = piece * SUBS
    per = n // PARTS
    has_u = x < NX - 1
    off_u = jnp.where(x == NX - 1, 0, jnp.where(x == NX - 2, LAGX, 2 * LAGX))
    off_b = jnp.where(x == NX - 1, LAGX, off_u)
    off_r = off_u + (nz - 1 - z) * LAG
    off_l = off_u + z * LAG
    off_f = jnp.maximum(off_r, off_l)

    def a_copy(k):
        return remote(a_out.at[k], a_in.at[k], a_ss.at[k], a_rs.at[k], {"segment": xl})

    def b_copy(k):
        return remote(b_out.at[k], b_in.at[k], b_ss.at[k], b_rs.at[k], {"segment": xr})

    def r_copy(k):
        return remote(r_out.at[k], r_in.at[k], r_ss.at[k], r_rs.at[k], {"segment": zl})

    def l_copy(k):
        return remote(l_out.at[k], l_in.at[k], l_ss.at[k], l_rs.at[k], {"segment": zr})

    def o_copy(k):
        r = k // (per * SUBS)
        col = (k - r * per * SUBS) * piece
        return pltpu.make_async_copy(
            acc.at[k],
            o_ref.at[pl.ds(pl.multiple_of(r * sub, sub), sub), pl.ds(pl.multiple_of(col, piece), piece)],
            o_sem.at[k])

    def contribution(k):
        r = k // per
        col = (k - r * per) * cols
        own = pl.ds(pl.multiple_of(h * half + col, cols), cols)
        oth = pl.ds(pl.multiple_of(col, cols), cols)
        at = pl.ds(pl.multiple_of(r * sub, sub), sub)
        return (fdot_t(grads[h, at, :2 * dim], wv_ref[own, :]) + fdot_t(grads[h, at, 2 * dim:], wk_ref[own, :])
                + fdot_t(grads[1 - h, at, :2 * dim], w_oth[1, oth, :])
                + fdot_t(grads[1 - h, at, 2 * dim:], w_oth[0, oth, :]))

    ends = (z == 0) | (z == nz - 1)

    def drain_sends():
        def drain(k, carry):
            @pl.when(x > 0)
            def _():
                a_copy(k).wait_send()

            @pl.when(x > 1)
            def _():
                b_copy(k).wait_send()

            @pl.when(z > 0)
            def _():
                r_copy(k).wait_send()

            @pl.when((z < nz - 1) & has_u)
            def _():
                l_copy(k).wait_send()
            return carry
        lax.fori_loop(0, pieces, drain, 0)
        for c in w_copies:
            c.wait_send()
        for p in range(PARTS):
            h_copy(p, h).wait_send()
            for q in range(2):
                for j in range(7):
                    rs_copy(j, p, q).wait_send()

        def drain_ctx(i, carry):
            for p in range(PIECES):
                up_copy(i, p).wait_send()

                @pl.when(i < 3)
                def _():
                    down_copy(i, p).wait_send()
            return carry
        lax.fori_loop(0, 4, drain_ctx, 0)

    def scan_step(t, carry):
        @pl.when(ends & (t == off_f - 2))
        def _():
            drain_sends()

        def turn(off, also=True):
            return (t >= off) & (t - off < n) & also

        def parts_of(off):
            return [(t - off) * SUBS + i for i in range(SUBS)]

        @pl.when(t < n)
        def _():
            c = contribution(t)
            for i, k in enumerate(parts_of(0)):
                d_buf[k] = c[:, i * piece:(i + 1) * piece]

            @pl.when((x == 3) | (x == 1))
            def _():
                for k in parts_of(0):
                    a_out[k] = d_buf[k].astype(BF16)
                    a_copy(k).start()

            @pl.when(x == 2)
            def _():
                for k in parts_of(0):
                    b_out[k] = d_buf[k].astype(BF16)
                    b_copy(k).start()

        @pl.when(turn(off_b, x == 3))
        def _():
            for k in parts_of(off_b):
                b_copy(k).wait_recv()
                b_out[k] = (d_buf[k] + b_in[k].astype(F32)).astype(BF16)
                b_copy(k).start()

        @pl.when(turn(off_u, x == 2))
        def _():
            for k in parts_of(off_u):
                a_copy(k).wait_recv()
                u_buf[k] = a_in[k].astype(F32)
                total = d_buf[k] + a_in[k].astype(F32)
                a_out[k] = total.astype(BF16)
                a_copy(k).start()
                d_buf[k] = total

        @pl.when(turn(off_u, x == 1))
        def _():
            for k in parts_of(off_u):
                a_copy(k).wait_recv()
                u_buf[k] = a_in[k].astype(F32)
                d_buf[k] = d_buf[k] + a_in[k].astype(F32)

        @pl.when(turn(off_u, x == 0))
        def _():
            for k in parts_of(off_u):
                a_copy(k).wait_recv()
                b_copy(k).wait_recv()
                u = a_in[k].astype(F32) + b_in[k].astype(F32)
                u_buf[k] = u
                d_buf[k] = d_buf[k] + u

        @pl.when(turn(off_r, z == nz - 1))
        def _():
            for k in parts_of(off_r):
                r_out[k] = d_buf[k].astype(BF16)
                r_copy(k).start()

        @pl.when(turn(off_r, (z > 0) & (z < nz - 1)))
        def _():
            for k in parts_of(off_r):
                r_copy(k).wait_recv()
                total = d_buf[k] + r_in[k].astype(F32)
                r_out[k] = total.astype(BF16)
                r_copy(k).start()

        @pl.when(turn(off_r, z == 0))
        def _():
            for k in parts_of(off_r):
                r_copy(k).wait_recv()

        @pl.when(turn(off_l, has_u & (z == 0)))
        def _():
            for k in parts_of(off_l):
                l_out[k] = u_buf[k].astype(BF16)
                l_copy(k).start()

        @pl.when(turn(off_l, has_u & (z > 0) & (z < nz - 1)))
        def _():
            for k in parts_of(off_l):
                l_copy(k).wait_recv()
                l_out[k] = (u_buf[k] + l_in[k].astype(F32)).astype(BF16)
                l_copy(k).start()

        @pl.when(turn(off_l, has_u & (z == nz - 1)))
        def _():
            for k in parts_of(off_l):
                l_copy(k).wait_recv()

        @pl.when(turn(off_f))
        def _():
            for k in parts_of(off_f):
                acc[k] = d_buf[k]

                @pl.when(z < nz - 1)
                def _():
                    acc[k] = acc[k] + r_in[k].astype(F32)

                @pl.when((z > 0) & has_u)
                def _():
                    acc[k] = acc[k] + l_in[k].astype(F32)
                o_copy(k).start()

                @pl.when(k >= HELD)
                def _():
                    o_copy(k - HELD).wait()
        return carry

    rs_final(0)
    for c in w_copies:
        c.wait_recv()
    for p in range(PARTS - 1):
        lax.fori_loop(p * per, (p + 1) * per, scan_step, 0)
        rs_final(p + 1)
    lax.fori_loop((PARTS - 1) * per, n + 2 * LAGX + (nz - 1) * LAG, scan_step, 0)

    @pl.when(jnp.logical_not(ends))
    def _():
        drain_sends()

    def drain_out(k, carry):
        o_copy(k).wait()
        return carry
    lax.fori_loop(pieces - HELD, pieces, drain_out, 0)


def per_device(nz, nctx, inputs, query, grad_out, w_key, w_value, keep_mask):
    tok, width = inputs.shape[1:]
    heads, dim = query.shape[2:]
    half = width // 2
    cols = COLS
    n = half // cols * PARTS
    sub = tok // PARTS
    rows = heads * tok // 2
    kv_cols = w_key.shape[2]
    major = lambda a: jnp.moveaxis(a[0], 1, 0).reshape(heads * tok, dim)
    dma = pltpu.SemaphoreType.DMA
    vmem = pl.BlockSpec(memory_space=pltpu.VMEM)
    hbm = pl.BlockSpec(memory_space=pltpu.HBM)
    nrs = 7 * PARTS * 2
    out = pl.pallas_call(
        functools.partial(kernel_body, nz, nctx),
        out_shape=jax.ShapeDtypeStruct((tok, half), F32),
        in_specs=[hbm, hbm, hbm, hbm, hbm, vmem],
        out_specs=pl.BlockSpec(memory_space=pl.ANY),
        scratch_shapes=[
            pltpu.VMEM((heads * tok, dim), BF16),
            pltpu.VMEM((heads * tok, dim), BF16),
            pltpu.VMEM((tok, width), BF16),
            pltpu.VMEM((width, kv_cols), BF16),
            pltpu.VMEM((width, kv_cols), BF16),
            pltpu.VMEM((nctx, 4, tok, dim), BF16),
            pltpu.VMEM((2, PARTS, nctx, sub, rows), F32),
            pltpu.VMEM((2, PARTS, nctx, sub, rows), F32),
            pltpu.VMEM((nctx, 2, 1, rows), F32),
            pltpu.VMEM((nctx, 2, 1, rows), F32),
            pltpu.VMEM((PARTS, 2, nctx, sub, 2 * dim), F32),
            pltpu.VMEM((nrs, sub, 2 * dim), BF16),
            pltpu.VMEM((nrs, sub, 2 * dim), BF16),
            pltpu.VMEM((2, tok, 4 * dim), BF16),
            pltpu.VMEM((2, half, 2 * dim), BF16),
        ] + [pltpu.VMEM((n * SUBS, sub, cols // SUBS), F32)] * 3 + [pltpu.VMEM((n * SUBS, sub, cols // SUBS), BF16)] * 8
        + [dma((15,)), dma((2,)), dma((8 * PIECES,)), dma((8 * PIECES,)), dma((nrs,)), dma((nrs,)), dma((2,)), dma((2,)), dma((PARTS,)), dma((PARTS,))]
        + [dma((n * SUBS,))] * 9,
        compiler_params=pltpu.CompilerParams(
            collective_id=0, has_side_effects=True, vmem_limit_bytes=VMEM_MIB * 2 ** 20),
        name="attention_backward_scan",
    )(inputs[0], major(query), major(grad_out), w_key[0], w_value[0], keep_mask.reshape(nctx, tok))
    return out[None]


def solution(mesh):
    return jax.shard_map(
        functools.partial(per_device, mesh.shape["segment"] // NX, mesh.shape["ctx"]),
        mesh=mesh,
        in_specs=(
            P("segment", "ctx", None),
            P("segment", "ctx", "head", None),
            P("segment", "ctx", "head", None),
            P("segment", None, "head"),
            P("segment", None, "head"),
            P(),
        ),
        out_specs=P("segment", "ctx", "head"),
        check_vma=False,
    )
```
